256 devices in a mesh: seq: 32 (over x, z), head: 8 (over y, core).
Axes of the slice: x: 4, y: 4, z: 8, core: 2. Of those that a mesh axis runs over, the one named last changes fastest.
Arguments:
- query: bfloat16 [32768, 4096], P('seq', 'head'), may hold values from -140 to 140
- key: bfloat16 [32768, 512], P('seq'), may hold values from -7 to 7
- value: bfloat16 [32768, 512], P('seq'), may hold values from -6 to 6
- out_grad: bfloat16 [32768, 4096], P('seq', 'head'), may hold values from -6 to 6
- chosen: int32 [32, 64, 4], P('head', 'seq'), may hold values from 0 to 63, as said below
- drop_seed: int32 [32], P('head'), may hold values from 0 to 16777215
Outputs:
- query_grad: float32 [32768, 4096], P('seq', 'head')
- key_grad: float32 [32768, 512], P(('seq', 'head'))
- value_grad: float32 [32768, 512], P(('seq', 'head'))
The draws below stay inside these ranges and needn't reach their ends.
Inputs may be any that keep to these rules, and one draw needn't show every extreme that they name: `chosen`: for head h and query block b, entry 0 is b; the other entries are distinct blocks before b whose shard lies at most 7 shards of 1024 tokens before the shard of b, or b itself where fewer such blocks exist.
All inputs are finite; a program needn't handle non-finite values.
Results may differ from the reference program's by a relative error of at most 0.014.
Values may be sent and summed in bfloat16 or wider, within the bound.
No kernel may reach another device: no remote copies, remote signals or barrier semaphores. Data moves between devices by JAX's collectives and lax.ppermute only.
A program may use at most 128 MiB of HBM per device.

```python
import jax
import jax.numpy as jnp
from jax import lax

HD = 128
HEADS = 32
KVH = 4
BLK = 512
TOPK = 4
TOK_DEV = 1024
WIN = 8
SEQ = 32768
NQB = 64


def key_field(key):
    raw = jnp.clip(jax.random.normal(jax.random.fold_in(key, 11), (SEQ, KVH * HD), jnp.float32), -6.0, 6.0)
    return raw


def draw_key(key, part):
    return key_field(key).astype(jnp.bfloat16)


def draw_query(key, part):
    base = jnp.clip(jax.random.normal(jax.random.fold_in(key, 13), (SEQ, HEADS * HD), jnp.float32), -6.0, 6.0)
    return base.astype(jnp.bfloat16)


def draw_chosen(key, part):
    per_shard = TOK_DEV // BLK
    width = WIN * per_shard
    block_ids = jnp.arange(NQB, dtype=jnp.int32)
    lowest = jnp.maximum(0, (block_ids // per_shard - WIN + 1) * per_shard)
    column = jnp.arange(width, dtype=jnp.int32)
    candidate = lowest[:, None] + column[None, :]
    usable = candidate < block_ids[:, None]
    draws = jax.random.randint(jax.random.fold_in(key, 21), (HEADS, NQB, width), 0, 1 << 20, dtype=jnp.int32)
    scores = jnp.where(usable[None], draws * width + column[None, None, :], -1 - column[None, None, :])
    picked_scores, picked_cols = lax.top_k(scores, TOPK - 1)
    picked = lowest[None, :, None] + picked_cols.astype(jnp.int32)
    picked = jnp.where(picked_scores >= 0, picked, block_ids[None, :, None])
    own = jnp.broadcast_to(block_ids[None, :, None], (HEADS, NQB, 1))
    return jnp.concatenate([own, picked], axis=2).astype(jnp.int32)


def with_ends(drawn, rng, low, high):
    index_at = [jax.random.randint(jax.random.fold_in(rng, axis), (), 0, length) for axis, length in enumerate(drawn.shape)]
    main_axis = drawn.shape.index(max(drawn.shape))
    beside = index_at[:main_axis] + [(index_at[main_axis] + 1) % drawn.shape[main_axis]] + index_at[main_axis + 1:]
    return drawn.at[tuple(index_at)].set(low).at[tuple(beside)].set(high)


def shard_levels(rng, shape, pieces, smallest, high):
    factor_of, own = 1.0, jax.random.fold_in(rng, 6)
    for dim, blocks in pieces:
        steps = jnp.exp(jax.random.uniform(jax.random.fold_in(own, dim), (blocks,), jnp.float32, smallest / len(pieces), high / len(pieces)))
        factor_of = factor_of * jnp.repeat(steps, shape[dim] // blocks).reshape([-1 if axis == dim else 1 for axis in range(len(shape))])
    return factor_of


def normal_values(own_key, extent, scale, most, split=(), held_as=jnp.bfloat16):
    gain = shard_levels(own_key, extent, split, -0.22, 0.18) if split else 1.0
    result = jax.random.normal(own_key, extent, jnp.float32) * scale * gain
    return jnp.minimum(jnp.maximum(result, -most), most).astype(held_as)


def setup_inputs(seed: int = 0) -> dict:
    streams_of = jax.random.split(jax.random.key(seed), 7)
    query = draw_query(jax.random.fold_in(streams_of[6], 71), 0)
    key = draw_key(jax.random.fold_in(streams_of[6], 71), 0)
    value = normal_values(streams_of[2], (SEQ, KVH * HD), 1.0, 6.0, ((0, 32),))
    out_grad = normal_values(streams_of[3], (SEQ, HEADS * HD), 1.0, 6.0, ((0, 32), (1, 8)))
    chosen = draw_chosen(jax.random.fold_in(streams_of[6], 71), 0)
    drop_seed = with_ends(jax.random.randint(streams_of[5], (HEADS,), 0, 16777216), jax.random.fold_in(streams_of[5], 1), 0, 16777215).astype(jnp.int32)
    return dict(query=query, key=key, value=value, out_grad=out_grad, chosen=chosen, drop_seed=drop_seed)


drop_cut = 6554
keep_gain = 1.0 / 0.9


def keep_scale(seed_value, query_pos, key_pos):
    mixed = seed_value + query_pos[:, None] * 40503 + key_pos[None, :] * 9973
    mixed = mixed ^ (jnp.right_shift(mixed, 15) & 131071)
    mixed = mixed * 73244475
    mixed = mixed ^ (jnp.right_shift(mixed, 13) & 524287)
    return jnp.where((mixed & 65535) >= drop_cut, keep_gain, 0.0).astype(jnp.float32)


def block_grads(query_block, out_block, key_sel, value_sel, query_pos, key_pos, allowed, seed_value):
    factor = key_sel.shape[-1] ** -0.5
    scores = jnp.dot(query_block, key_sel.T, preferred_element_type=jnp.float32) * factor
    scores = jnp.where(allowed, scores, -jnp.inf)
    peak = jnp.max(scores, axis=1, keepdims=True)
    total = jnp.sum(jnp.exp(scores - peak), axis=1, keepdims=True)
    probs = jnp.exp(scores - (peak + jnp.log(total)))
    gains = keep_scale(seed_value, query_pos, key_pos)
    dropped = (probs * gains).astype(jnp.bfloat16)
    output = jnp.dot(dropped, value_sel, preferred_element_type=jnp.float32)
    delta = jnp.sum(out_block.astype(jnp.float32) * output, axis=1, keepdims=True)
    pgrad = jnp.dot(out_block, value_sel.T, preferred_element_type=jnp.float32)
    sgrad = (probs * (pgrad * gains - delta)).astype(jnp.bfloat16)
    qgrad = jnp.dot(sgrad, key_sel, preferred_element_type=jnp.float32) * factor
    kgrad = jnp.dot(sgrad.T, query_block, preferred_element_type=jnp.float32) * factor
    vgrad = jnp.dot(dropped.T, out_block, preferred_element_type=jnp.float32)
    return qgrad, kgrad, vgrad


def reference(query, key, value, out_grad, chosen, drop_seed):
    seq_len = query.shape[0]
    blocks = seq_len // BLK
    group = HEADS // KVH
    head_list = jnp.repeat(jnp.arange(HEADS, dtype=jnp.int32), blocks)
    block_list = jnp.tile(jnp.arange(blocks, dtype=jnp.int32), HEADS)
    lists = chosen.reshape(HEADS * blocks, TOPK).astype(jnp.int32)
    seeds = jnp.repeat(drop_seed, blocks).astype(jnp.int32)
    offsets = jnp.arange(BLK, dtype=jnp.int32)

    def visit(carry, item):
        key_grad, value_grad = carry
        head, block, picks, seed_value = item
        kv_col = ((head // group) * HD).astype(jnp.int32)
        query_rows = (block * BLK).astype(jnp.int32)
        query_block = lax.dynamic_slice(query, (query_rows, (head * HD).astype(jnp.int32)), (BLK, HD))
        out_block = lax.dynamic_slice(out_grad, (query_rows, (head * HD).astype(jnp.int32)), (BLK, HD))
        key_parts, value_parts, pos_parts, live_parts = [], [], [], []
        for entry in range(TOPK):
            start = (picks[entry] * BLK).astype(jnp.int32)
            key_parts.append(lax.dynamic_slice(key, (start, kv_col), (BLK, HD)))
            value_parts.append(lax.dynamic_slice(value, (start, kv_col), (BLK, HD)))
            pos_parts.append(start + offsets)
            if entry == 0:
                fresh = jnp.ones((BLK,), dtype=bool)
            else:
                fresh = jnp.broadcast_to(jnp.logical_not(jnp.any(picks[:entry] == picks[entry])), (BLK,))
            live_parts.append(fresh)
        key_pos = jnp.concatenate(pos_parts)
        query_pos = query_rows + offsets
        allowed = (key_pos[None, :] <= query_pos[:, None]) & jnp.concatenate(live_parts)[None, :]
        qgrad, kgrad, vgrad = block_grads(query_block, out_block, jnp.concatenate(key_parts), jnp.concatenate(value_parts), query_pos, key_pos, allowed, seed_value)
        for entry in range(TOPK):
            start = (picks[entry] * BLK).astype(jnp.int32)
            old_key = lax.dynamic_slice(key_grad, (start, kv_col), (BLK, HD))
            key_grad = lax.dynamic_update_slice(key_grad, old_key + kgrad[entry * BLK:(entry + 1) * BLK], (start, kv_col))
            old_value = lax.dynamic_slice(value_grad, (start, kv_col), (BLK, HD))
            value_grad = lax.dynamic_update_slice(value_grad, old_value + vgrad[entry * BLK:(entry + 1) * BLK], (start, kv_col))
        return (key_grad, value_grad), qgrad

    empty = jnp.zeros((seq_len, KVH * HD), jnp.float32)
    (key_grad, value_grad), qgrads = lax.scan(visit, (empty, empty), (head_list, block_list, lists, seeds))
    query_grad = qgrads.reshape(HEADS, blocks, BLK, HD).transpose(1, 2, 0, 3).reshape(seq_len, HEADS * HD)
    return query_grad, key_grad, value_grad
```

```python
import functools

import jax
import jax.numpy as jnp
import numpy as np
from jax import lax
from jax.experimental import pallas as pl
from jax.experimental.pallas import tpu as pltpu
from jax.sharding import Mesh
from jax.sharding import PartitionSpec as P

HD = 128
BLK = 512
TOPK = 4
SLOTS = 8
ITEMS = 8
ROWS = 1024
DROP_CUT = 6554
LOG2E = 1.4426950408889634
FACTOR = HD**-0.5
SEQ_AXES = ("x", "z")
SEQ_SIZE = 32


def nt_dot(lhs, rhs):
    return lax.dot_general(lhs, rhs, (((1,), (1,)), ((), ())), preferred_element_type=jnp.float32)


def tn_dot(lhs, rhs):
    return lax.dot_general(lhs, rhs, (((0,), (0,)), ((), ())), preferred_element_type=jnp.float32)


def nn_dot(lhs, rhs):
    return lax.dot_general(lhs, rhs, (((1,), (0,)), ((), ())), preferred_element_type=jnp.float32)


def grads_kernel(
    picks, seeds, place, query, out_grad, *rest
):
    pieces = rest[:16]
    query_grad, keep, send = rest[16:19]
    kv, acc, table, signed, kept, dropped_ref, sems = rest[19:]
    item = pl.program_id(0)
    shard = place[0]
    core = place[1]
    head = item // 2
    block = item % 2

    def copies():
        made = []
        for slot in range(SLOTS):
            for half in range(2):
                if slot == 0:
                    kind = half
                else:
                    kind = core if half == 0 else 1 - core
                made.append(
                    pltpu.make_async_copy(
                        pieces[2 * slot + half], kv.at[slot, kind], sems.at[2 * slot + half]
                    )
                )
        return made

    @pl.when(item == 0)
    def _():
        made = copies()
        for copy in made:
            copy.start()
        acc[...] = jnp.zeros_like(acc)
        key_row = lax.broadcasted_iota(jnp.int32, (BLK, BLK), 0)
        query_row = lax.broadcasted_iota(jnp.int32, (BLK, BLK), 1)
        table[...] = (key_row * 9973 + query_row * 40503).astype(jnp.uint32)
        for copy in made:
            copy.wait()

    own = shard * 2 + block
    q = query[...]
    do = out_grad[...]

    def target_of(entry):
        return picks[item, entry]

    dead = [jnp.bool_(False)]
    for entry in range(1, TOPK):
        same = target_of(entry) == target_of(0)
        for other in range(1, entry):
            same = same | (target_of(entry) == target_of(other))
        dead.append(same)

    def kv_rows(entry, kind):
        target = target_of(entry)
        slot = shard - target // 2
        start = pl.multiple_of((target % 2) * BLK, BLK)
        return kv[slot, kind, pl.ds(start, BLK), :]

    def unit_rows(entry, chunk, kind):
        target = target_of(entry)
        slot = shard - target // 2
        start = pl.multiple_of((target % 2) * BLK + chunk * 256, 256)
        return kv[slot, kind, pl.ds(start, 256), :]

    def first_query(entry, chunk):
        return chunk * 256 if entry == 0 else 0

    def fold(value, how):
        return how(value.reshape(256 // 8, 8, value.shape[1]), axis=0)

    units = [(entry, chunk) for entry in range(TOPK) for chunk in range(BLK // 256)]

    def score_dot(entry, chunk):
        lo = first_query(entry, chunk)
        return nt_dot(unit_rows(entry, chunk, 0), q[lo:])

    def widen(value, lo, fill):
        if lo == 0:
            return value
        return jnp.concatenate([jnp.full((8, lo), fill, jnp.float32), value], axis=1)

    def score_rest(entry, chunk, value):
        lo = first_query(entry, chunk)
        if entry == 0:
            key_row = lax.broadcasted_iota(jnp.int32, value.shape, 0)
            query_row = lax.broadcasted_iota(jnp.int32, value.shape, 1)
            value = jnp.where(key_row <= query_row, value, -jnp.inf)
        signed[entry, chunk * 256:(chunk + 1) * 256, lo:] = value
        top = widen(fold(value, jnp.max), lo, -jnp.inf)
        return jnp.where(dead[entry], -jnp.inf, top) if entry else top

    peak = jnp.full((8, BLK), -jnp.inf, jnp.float32)
    ahead = score_dot(*units[0])
    for place_in, unit in enumerate(units):
        value = ahead
        if place_in + 1 < len(units):
            ahead = score_dot(*units[place_in + 1])
        peak = jnp.maximum(peak, score_rest(*unit, value))
    peak = jnp.max(peak, axis=0, keepdims=True)

    def middle_dot(entry, chunk):
        lo = first_query(entry, chunk)
        return nt_dot(unit_rows(entry, chunk, 1), do[lo:])

    def middle_rest(entry, chunk, pgrad):
        lo = first_query(entry, chunk)
        rows = slice(chunk * 256, (chunk + 1) * 256)
        top = peak[:, lo:]
        if entry:
            top = jnp.where(dead[entry], jnp.inf, top)
        e = jnp.exp2((signed[entry, rows, lo:] - top) * (FACTOR * LOG2E))
        base = seeds[head] + own * (BLK * 40503) + target_of(entry) * (BLK * 9973)
        x = table[rows, lo:] + base.astype(jnp.uint32)
        x = x ^ lax.shift_right_logical(x, jnp.uint32(15))
        x = (x * np.uint32((73244475 << 16) % 2**32)) ^ (x * np.uint32((73244475 << 3) % 2**32))
        keeps = x >= np.uint32(DROP_CUT << 16)
        pk = jnp.where(keeps, pgrad, 0.0)
        signed[entry, rows, lo:] = e
        dropped_ref[entry, rows, lo:] = jnp.where(keeps, e, 0.0).astype(jnp.bfloat16)
        kept[entry, rows, lo:] = pk
        return widen(fold(e, jnp.sum), lo, 0.0), widen(fold(e * pk, jnp.sum), lo, 0.0)

    total = delta = jnp.zeros((8, BLK), jnp.float32)
    ahead = middle_dot(*units[0])
    for place_in, unit in enumerate(units):
        value = ahead
        if place_in + 1 < len(units):
            ahead = middle_dot(*units[place_in + 1])
        more_total, more_delta = middle_rest(*unit, value)
        total = total + more_total
        delta = delta + more_delta
    total = jnp.sum(total, axis=0, keepdims=True)
    delta = jnp.sum(delta, axis=0, keepdims=True) / total
    scale = 1.0 / (0.9 * total)
    scale_cols = jnp.transpose(jnp.broadcast_to(scale, (HD, BLK)))
    q_scaled = (q.astype(jnp.float32) * (scale_cols * FACTOR)).astype(jnp.bfloat16)
    do_scaled = (do.astype(jnp.float32) * scale_cols).astype(jnp.bfloat16)

    def last_rest(entry, chunk):
        lo = first_query(entry, chunk)
        rows = slice(chunk * 256, (chunk + 1) * 256)
        sgrad = (signed[entry, rows, lo:] * (kept[entry, rows, lo:] - delta[:, lo:])).astype(jnp.bfloat16)
        return sgrad, dropped_ref[entry, rows, lo:]

    def last_dots(entry, chunk, sgrad, dropped, qgrad):
        lo = first_query(entry, chunk)
        target = target_of(entry)
        slot = shard - target // 2
        part = (target % 2) * 2 + chunk * (256 // 256)
        shape = (256 // 256, 2, 128, HD)
        acc[slot, 0, pl.ds(part, 256 // 256)] += nn_dot(sgrad, q_scaled[lo:]).reshape(shape)
        acc[slot, 1, pl.ds(part, 256 // 256)] += nn_dot(dropped, do_scaled[lo:]).reshape(shape)
        more = tn_dot(unit_rows(entry, chunk, 0), sgrad)
        if lo:
            return jnp.concatenate([qgrad[:, :lo], qgrad[:, lo:] + more], axis=1)
        return qgrad + more

    qgrad = jnp.zeros((HD, BLK), jnp.float32)
    ahead = last_rest(*units[0])
    for place_in, unit in enumerate(units):
        value = ahead
        if place_in + 1 < len(units):
            ahead = last_rest(*units[place_in + 1])
        qgrad = last_dots(*unit, *value, qgrad)
    query_grad[...] = jnp.transpose(qgrad * (scale * FACTOR))

    @pl.when(item == ITEMS - 1)
    def _():
        for slot in range(SLOTS):
            keep[slot] = acc[slot, :, :, core]
            send[slot] = acc[slot, :, :, 1 - core].astype(jnp.bfloat16)


def block_grads(query, out_grad, picks, seeds, place, pieces, interpret=False):
    any_spec = pl.BlockSpec(memory_space=pl.ANY)
    item_spec = pl.BlockSpec((BLK, HD), lambda i, *_: (i % 2, i // 2))
    part_spec = pl.BlockSpec((SLOTS, 2, 4, 128, HD), lambda i, *_: (0, 0, 0, 0, 0))
    part_shape = jax.ShapeDtypeStruct((SLOTS, 2, 4, 128, HD), jnp.bfloat16)
    return pl.pallas_call(
        grads_kernel,
        grid_spec=pltpu.PrefetchScalarGridSpec(
            num_scalar_prefetch=3,
            grid=(ITEMS,),
            in_specs=[item_spec, item_spec] + [any_spec] * 16,
            out_specs=[item_spec, part_spec, part_spec],
            scratch_shapes=[
                pltpu.VMEM((SLOTS, 2, ROWS, HD), jnp.bfloat16),
                pltpu.VMEM((SLOTS, 2, 4, 2, 128, HD), jnp.float32),
                pltpu.VMEM((BLK, BLK), jnp.uint32),
                pltpu.VMEM((TOPK, BLK, BLK), jnp.float32),
                pltpu.VMEM((TOPK, BLK, BLK), jnp.float32),
                pltpu.VMEM((TOPK, BLK, BLK), jnp.bfloat16),
                pltpu.SemaphoreType.DMA((16,)),
            ],
        ),
        out_shape=[
            jax.ShapeDtypeStruct((ROWS, 4 * HD), jnp.float32),
            jax.ShapeDtypeStruct((SLOTS, 2, 4, 128, HD), jnp.float32),
            part_shape,
        ],
        compiler_params=pltpu.CompilerParams(
            vmem_limit_bytes=56 * 1024 * 1024, dimension_semantics=("arbitrary",)
        ),
        name="block_grads",
        interpret=interpret,
    )(picks, seeds, place, query, out_grad, *pieces)


def shifted(array, by):
    pairs = [(i, (i + by) % SEQ_SIZE) for i in range(SEQ_SIZE)]
    return lax.ppermute(array, SEQ_AXES, pairs)


def swapped(array):
    return lax.ppermute(array, "core", [(0, 1), (1, 0)])


def local(query, key, value, out_grad, chosen, drop_seed):
    shard = lax.axis_index(SEQ_AXES)
    core = lax.axis_index("core")
    kv_col = lax.axis_index("y") * HD
    own_key = lax.dynamic_slice_in_dim(key, kv_col, HD, 1)
    own_value = lax.dynamic_slice_in_dim(value, kv_col, HD, 1)
    mine = jnp.where(core == 0, own_key, own_value)
    half = ROWS // 2
    got = {}
    got[1] = shifted(mine, 1)
    got[7] = shifted(mine, 7)
    got[2] = shifted(got[1], 1)
    got[6] = shifted(got[7], -1)
    low = shifted(got[2][:half], 2)
    high = shifted(got[6][half:], -2)
    got[3] = shifted(got[2], 1)
    got[5] = shifted(got[6], -1)
    got[4] = jnp.concatenate([low, high])
    pieces = [own_key, own_value]
    for slot in range(1, SLOTS):
        pieces += [got[slot], swapped(got[slot])]
    place = jnp.stack([shard, core]).astype(jnp.int32)
    query_grad, keep, send = block_grads(
        query, out_grad, chosen.reshape(ITEMS, TOPK), drop_seed, place, pieces
    )
    other = swapped(send)

    def total(slot, *more):
        return sum((p.astype(jnp.float32) for p in more), keep[slot] + other[slot].astype(jnp.float32))

    def rounded(array):
        return array.astype(jnp.bfloat16)

    sent4 = rounded(total(4))
    from3 = shifted(rounded(total(3)), -1)
    from5 = shifted(rounded(total(5)), 1)
    from4k = shifted(sent4[0], -2)
    from4v = shifted(sent4[1], 2)
    none = jnp.zeros_like(from4k)
    part2 = rounded(total(2, from3, jnp.stack([from4k, none])))
    part6 = rounded(total(6, from5, jnp.stack([none, from4v])))
    part1 = rounded(total(1, shifted(part2, -1)))
    part7 = rounded(total(7, shifted(part6, 1)))
    summed = rounded(total(0, shifted(part1, -1), shifted(part7, -7)))
    spread = lax.all_to_all(summed, "y", 1, 1, tiled=True)
    spread = jnp.transpose(spread.astype(jnp.float32), (0, 2, 1, 3)).reshape(2, 128, 4 * HD)
    return query_grad, spread[0], spread[1]


def solution(mesh):
    fine = Mesh(mesh.devices.reshape(4, 8, 4, 2), ("x", "z", "y", "core"))
    seq, head = SEQ_AXES, ("y", "core")
    in_specs = (
        P(seq, head),
        P(seq, None),
        P(seq, None),
        P(seq, head),
        P(head, seq, None),
        P(head),
    )
    out_specs = (P(seq, head), P(seq + head, None), P(seq + head, None))
    return jax.shard_map(local, mesh=fine, in_specs=in_specs, out_specs=out_specs, check_vma=False)
```

```python
import functools

import jax
import jax.numpy as jnp
import numpy as np
from jax import lax
from jax.experimental import pallas as pl
from jax.experimental.pallas import tpu as pltpu
from jax.sharding import Mesh
from jax.sharding import PartitionSpec as P

HD = 128
BLK = 512
TOPK = 4
SLOTS = 8
ITEMS = 8
ROWS = 1024
DROP_CUT = 6554
LOG2E = 1.4426950408889634
FACTOR = HD**-0.5
SEQ_AXES = ("x", "z")
SEQ_SIZE = 32
Y_SIZE = 4
FAR = (3, 4, 5)
NEAR = (0, 1, 2, 6, 7)


def nt_dot(lhs, rhs):
    return lax.dot_general(lhs, rhs, (((1,), (1,)), ((), ())), preferred_element_type=jnp.float32)


def tn_dot(lhs, rhs):
    return lax.dot_general(lhs, rhs, (((0,), (0,)), ((), ())), preferred_element_type=jnp.float32)


def nn_dot(lhs, rhs):
    return lax.dot_general(lhs, rhs, (((1,), (0,)), ((), ())), preferred_element_type=jnp.float32)


def grads_kernel(
    picks, seeds, place, query, out_grad, *rest
):
    pieces = rest[:16]
    query_grad, keep, send_far, send_near = rest[16:20]
    kv, acc, table, signed, kept, dropped_ref, sems = rest[20:]
    item = pl.program_id(0)
    shard = place[0]
    core = place[1]
    head = item // 2
    block = item % 2

    def copies():
        made = []
        for slot in range(SLOTS):
            for half in range(2):
                if slot == 0:
                    kind = half
                else:
                    kind = core if half == 0 else 1 - core
                source = pieces[2 * slot + half]
                if slot == 0:
                    source = source.at[:, pl.ds(pl.multiple_of(place[2], HD), HD)]
                made.append(
                    pltpu.make_async_copy(source, kv.at[slot, kind], sems.at[2 * slot + half])
                )
        return made

    @pl.when(item == 0)
    def _():
        made = copies()
        for copy in made:
            copy.start()
        acc[...] = jnp.zeros_like(acc)
        key_row = lax.broadcasted_iota(jnp.int32, (BLK, BLK), 0)
        query_row = lax.broadcasted_iota(jnp.int32, (BLK, BLK), 1)
        table[...] = (key_row * 9973 + query_row * 40503).astype(jnp.uint32)
        for copy in made:
            copy.wait()

    own = shard * 2 + block
    q = query[...]
    do = out_grad[...]

    def target_of(entry):
        return picks[item, entry]

    dead = [jnp.bool_(False)]
    for entry in range(1, TOPK):
        same = target_of(entry) == target_of(0)
        for other in range(1, entry):
            same = same | (target_of(entry) == target_of(other))
        dead.append(same)

    def kv_rows(entry, kind):
        target = target_of(entry)
        slot = shard - target // 2
        start = pl.multiple_of((target % 2) * BLK, BLK)
        return kv[slot, kind, pl.ds(start, BLK), :]

    def unit_rows(entry, chunk, kind):
        target = target_of(entry)
        slot = shard - target // 2
        start = pl.multiple_of((target % 2) * BLK + chunk * 256, 256)
        return kv[slot, kind, pl.ds(start, 256), :]

    def first_query(entry, chunk):
        return chunk * 256 if entry == 0 else 0

    def fold(value, how):
        return how(value.reshape(256 // 8, 8, value.shape[1]), axis=0)

    units = [(entry, chunk) for entry in range(TOPK) for chunk in range(BLK // 256)]

    def score_dot(entry, chunk):
        lo = first_query(entry, chunk)
        return nt_dot(unit_rows(entry, chunk, 0), q[lo:])

    def widen(value, lo, fill):
        if lo == 0:
            return value
        return jnp.concatenate([jnp.full((8, lo), fill, jnp.float32), value], axis=1)

    def score_rest(entry, chunk, value):
        lo = first_query(entry, chunk)
        if entry == 0:
            key_row = lax.broadcasted_iota(jnp.int32, value.shape, 0)
            query_row = lax.broadcasted_iota(jnp.int32, value.shape, 1)
            value = jnp.where(key_row <= query_row, value, -jnp.inf)
        signed[entry, chunk * 256:(chunk + 1) * 256, lo:] = value
        top = widen(fold(value, jnp.max), lo, -jnp.inf)
        return jnp.where(dead[entry], -jnp.inf, top) if entry else top

    peak = jnp.full((8, BLK), -jnp.inf, jnp.float32)
    ahead = score_dot(*units[0])
    for place_in, unit in enumerate(units):
        value = ahead
        if place_in + 1 < len(units):
            ahead = score_dot(*units[place_in + 1])
        peak = jnp.maximum(peak, score_rest(*unit, value))
    peak = jnp.max(peak, axis=0, keepdims=True)

    def middle_dot(entry, chunk):
        lo = first_query(entry, chunk)
        return nt_dot(unit_rows(entry, chunk, 1), do[lo:])

    def middle_rest(entry, chunk, pgrad):
        lo = first_query(entry, chunk)
        rows = slice(chunk * 256, (chunk + 1) * 256)
        top = peak[:, lo:]
        if entry:
            top = jnp.where(dead[entry], jnp.inf, top)
        e = jnp.exp2((signed[entry, rows, lo:] - top) * (FACTOR * LOG2E))
        base = seeds[head] + own * (BLK * 40503) + target_of(entry) * (BLK * 9973)
        x = table[rows, lo:] + base.astype(jnp.uint32)
        x = x ^ lax.shift_right_logical(x, jnp.uint32(15))
        x = (x * np.uint32((73244475 << 16) % 2**32)) ^ (x * np.uint32((73244475 << 3) % 2**32))
        keeps = x >= np.uint32(DROP_CUT << 16)
        pk = jnp.where(keeps, pgrad, 0.0)
        signed[entry, rows, lo:] = e
        dropped_ref[entry, rows, lo:] = jnp.where(keeps, e, 0.0).astype(jnp.bfloat16)
        kept[entry, rows, lo:] = pk
        return widen(fold(e, jnp.sum), lo, 0.0), widen(fold(e * pk, jnp.sum), lo, 0.0)

    total = delta = jnp.zeros((8, BLK), jnp.float32)
    ahead = middle_dot(*units[0])
    for place_in, unit in enumerate(units):
        value = ahead
        if place_in + 1 < len(units):
            ahead = middle_dot(*units[place_in + 1])
        more_total, more_delta = middle_rest(*unit, value)
        total = total + more_total
        delta = delta + more_delta
    total = jnp.sum(total, axis=0, keepdims=True)
    delta = jnp.sum(delta, axis=0, keepdims=True) / total
    scale = 1.0 / (0.9 * total)
    scale_cols = jnp.transpose(jnp.broadcast_to(scale, (HD, BLK)))
    q_scaled = (q.astype(jnp.float32) * (scale_cols * FACTOR)).astype(jnp.bfloat16)
    do_scaled = (do.astype(jnp.float32) * scale_cols).astype(jnp.bfloat16)

    def last_rest(entry, chunk):
        lo = first_query(entry, chunk)
        rows = slice(chunk * 256, (chunk + 1) * 256)
        sgrad = (signed[entry, rows, lo:] * (kept[entry, rows, lo:] - delta[:, lo:])).astype(jnp.bfloat16)
        return sgrad, dropped_ref[entry, rows, lo:]

    def last_dots(entry, chunk, sgrad, dropped, qgrad):
        lo = first_query(entry, chunk)
        target = target_of(entry)
        slot = shard - target // 2
        part = (target % 2) * 2 + chunk * (256 // 256)
        shape = (256 // 256, 2, 128, HD)
        acc[slot, 0, pl.ds(part, 256 // 256)] += nn_dot(sgrad, q_scaled[lo:]).reshape(shape)
        acc[slot, 1, pl.ds(part, 256 // 256)] += nn_dot(dropped, do_scaled[lo:]).reshape(shape)
        more = tn_dot(unit_rows(entry, chunk, 0), sgrad)
        if lo:
            return jnp.concatenate([qgrad[:, :lo], qgrad[:, lo:] + more], axis=1)
        return qgrad + more

    qgrad = jnp.zeros((HD, BLK), jnp.float32)
    ahead = last_rest(*units[0])
    for place_in, unit in enumerate(units):
        value = ahead
        if place_in + 1 < len(units):
            ahead = last_rest(*units[place_in + 1])
        qgrad = last_dots(*unit, *value, qgrad)
    query_grad[...] = jnp.transpose(qgrad * (scale * FACTOR))

    @pl.when(item == ITEMS - 1)
    def _():
        for slot in range(SLOTS):
            keep[slot] = acc[slot, :, :, core]
            group = send_far if slot in FAR else send_near
            index = (FAR if slot in FAR else NEAR).index(slot)
            group[index] = acc[slot, :, :, 1 - core].astype(jnp.bfloat16)


def block_grads(query, out_grad, picks, seeds, place, pieces, interpret=False):
    any_spec = pl.BlockSpec(memory_space=pl.ANY)
    item_spec = pl.BlockSpec((BLK, HD), lambda i, *_: (i % 2, i // 2))

    def part(slots, dtype):
        shape = (slots, 2, Y_SIZE, 128, HD)
        return pl.BlockSpec(shape, lambda i, *_: (0, 0, 0, 0, 0)), jax.ShapeDtypeStruct(shape, dtype)

    parts = [
        part(SLOTS, jnp.float32),
        part(len(FAR), jnp.bfloat16),
        part(len(NEAR), jnp.bfloat16),
    ]
    return pl.pallas_call(
        grads_kernel,
        grid_spec=pltpu.PrefetchScalarGridSpec(
            num_scalar_prefetch=3,
            grid=(ITEMS,),
            in_specs=[item_spec, item_spec] + [any_spec] * 16,
            out_specs=[item_spec] + [spec for spec, _ in parts],
            scratch_shapes=[
                pltpu.VMEM((SLOTS, 2, ROWS, HD), jnp.bfloat16),
                pltpu.VMEM((SLOTS, 2, 4, 2, 128, HD), jnp.float32),
                pltpu.VMEM((BLK, BLK), jnp.uint32),
                pltpu.VMEM((TOPK, BLK, BLK), jnp.float32),
                pltpu.VMEM((TOPK, BLK, BLK), jnp.float32),
                pltpu.VMEM((TOPK, BLK, BLK), jnp.bfloat16),
                pltpu.SemaphoreType.DMA((16,)),
            ],
        ),
        out_shape=[jax.ShapeDtypeStruct((ROWS, 4 * HD), jnp.float32)]
        + [shape for _, shape in parts],
        compiler_params=pltpu.CompilerParams(
            vmem_limit_bytes=56 * 1024 * 1024, dimension_semantics=("arbitrary",)
        ),
        name="block_grads",
        interpret=interpret,
    )(picks, seeds, place, query, out_grad, *pieces)


def shifted(array, by):
    pairs = [(i, (i + by) % SEQ_SIZE) for i in range(SEQ_SIZE)]
    return lax.ppermute(array, SEQ_AXES, pairs)


def swapped(array):
    return lax.ppermute(array, "core", [(0, 1), (1, 0)])


def own_kernel(where, keep, other, low, high, *outs):
    for offset in range(Y_SIZE):
        rows = lax.rem(where[0] + offset, Y_SIZE)
        value = keep[0, :, rows] + other[0, :, rows].astype(jnp.float32)
        value = value + low[:, rows].astype(jnp.float32) + high[:, rows].astype(jnp.float32)
        outs[offset][...] = value.astype(outs[offset].dtype)


def own_sums(where, keep, other, low, high):
    def first(count):
        return pl.BlockSpec((count, 2, Y_SIZE, 128, HD), lambda i, *_: (0, 0, 0, 0, 0))

    whole = pl.BlockSpec((2, Y_SIZE, 128, HD), lambda i, *_: (0, 0, 0, 0))
    out = pl.BlockSpec((2, 128, HD), lambda i, *_: (0, 0, 0))
    return pl.pallas_call(
        own_kernel,
        grid_spec=pltpu.PrefetchScalarGridSpec(
            num_scalar_prefetch=1,
            grid=(1,),
            in_specs=[first(1), first(1), whole, whole],
            out_specs=[out] * Y_SIZE,
        ),
        out_shape=[
            jax.ShapeDtypeStruct((2, 128, HD), jnp.bfloat16 if offset else jnp.float32)
            for offset in range(Y_SIZE)
        ],
        name="own_sums",
    )(where, keep, other, low, high)


def spread_kernel(where, *refs):
    key_grad, value_grad = refs[Y_SIZE:]
    for offset in range(Y_SIZE):
        start = pl.multiple_of(lax.rem(where[0] + Y_SIZE - offset, Y_SIZE) * HD, HD)
        key_grad[:, pl.ds(start, HD)] = refs[offset][0].astype(jnp.float32)
        value_grad[:, pl.ds(start, HD)] = refs[offset][1].astype(jnp.float32)


def spread(where, pieces):
    piece = pl.BlockSpec((2, 128, HD), lambda i, *_: (0, 0, 0))
    out = pl.BlockSpec((128, Y_SIZE * HD), lambda i, *_: (0, 0))
    return pl.pallas_call(
        spread_kernel,
        grid_spec=pltpu.PrefetchScalarGridSpec(
            num_scalar_prefetch=1,
            grid=(1,),
            in_specs=[piece] * Y_SIZE,
            out_specs=[out, out],
        ),
        out_shape=[jax.ShapeDtypeStruct((128, Y_SIZE * HD), jnp.float32)] * 2,
        name="spread",
    )(where, *pieces)


def local(query, key, value, out_grad, chosen, drop_seed):
    shard = lax.axis_index(SEQ_AXES)
    core = lax.axis_index("core")
    rank = lax.axis_index("y")
    kv_col = rank * HD
    mine = jnp.where(
        core == 0,
        lax.dynamic_slice_in_dim(key, kv_col, HD, 1),
        lax.dynamic_slice_in_dim(value, kv_col, HD, 1),
    )
    half = ROWS // 2
    got = {}
    got[1] = shifted(mine, 1)
    got[7] = shifted(mine, 7)
    got[2] = shifted(got[1], 1)
    got[6] = shifted(got[7], -1)
    low = shifted(got[2][:half], 2)
    high = shifted(got[6][half:], -2)
    got[3] = shifted(got[2], 1)
    got[5] = shifted(got[6], -1)
    got[4] = jnp.concatenate([low, high])
    pieces = [key, value]
    for slot in range(1, SLOTS):
        pieces += [got[slot], swapped(got[slot])]
    place = jnp.stack([shard, core, kv_col]).astype(jnp.int32)
    query_grad, keep, send_far, send_near = block_grads(
        query, out_grad, chosen.reshape(ITEMS, TOPK), drop_seed, place, pieces
    )
    far = swapped(send_far)
    near = swapped(send_near)

    def total(slot, *more):
        other = far[FAR.index(slot)] if slot in FAR else near[NEAR.index(slot)]
        return sum((p.astype(jnp.float32) for p in more), keep[slot] + other.astype(jnp.float32))

    def rounded(array):
        return array.astype(jnp.bfloat16)

    sent3, sent5, sent4k, sent4v = lax.optimization_barrier(
        (rounded(total(3)), rounded(total(5)), rounded(total(4)[0]), rounded(total(4)[1]))
    )
    from3 = shifted(sent3, -1)
    from5 = shifted(sent5, 1)
    from4k = shifted(sent4k, -2)
    from4v = shifted(sent4v, 2)
    none = jnp.zeros_like(from4k)
    part2 = rounded(total(2, from3, jnp.stack([from4k, none])))
    part6 = rounded(total(6, from5, jnp.stack([none, from4v])))
    part2, part6 = lax.optimization_barrier((part2, part6))
    part1 = rounded(total(1, shifted(part2, -1)))
    part7 = rounded(total(7, shifted(part6, 1)))
    part1, part7 = lax.optimization_barrier((part1, part7))
    from1, from7 = shifted(part1, -1), shifted(part7, -7)
    where = rank.astype(jnp.int32).reshape(1)
    sums = own_sums(where, keep, near, from1, from7)
    pieces = [sums[0]]
    for offset in range(1, Y_SIZE):
        pairs = [(i, (i + offset) % Y_SIZE) for i in range(Y_SIZE)]
        pieces.append(lax.ppermute(sums[offset], "y", pairs))
    key_grad, value_grad = spread(where, pieces)
    return query_grad, key_grad, value_grad


def solution(mesh):
    fine = Mesh(mesh.devices.reshape(4, 8, 4, 2), ("x", "z", "y", "core"))
    seq, head = SEQ_AXES, ("y", "core")
    in_specs = (
        P(seq, head),
        P(seq, None),
        P(seq, None),
        P(seq, head),
        P(head, seq, None),
        P(head),
    )
    out_specs = (P(seq, head), P(seq + head, None), P(seq + head, None))
    return jax.shard_map(local, mesh=fine, in_specs=in_specs, out_specs=out_specs, check_vma=False)
```

```python
import functools

import jax
import jax.numpy as jnp
import numpy as np
from jax import lax
from jax.experimental import pallas as pl
from jax.experimental.pallas import tpu as pltpu
from jax.sharding import Mesh
from jax.sharding import PartitionSpec as P

HD = 128
BLK = 512
TOPK = 4
SLOTS = 8
ITEMS = 8
ROWS = 1024
DROP_CUT = 6554
LOG2E = 1.4426950408889634
FACTOR = HD**-0.5
SEQ_AXES = ("x", "z")
SEQ_SIZE = 32
Y_SIZE = 4
FAR = (3, 4, 5)
NEAR = (0, 1, 2, 6, 7)


def nt_dot(lhs, rhs):
    return lax.dot_general(lhs, rhs, (((1,), (1,)), ((), ())), preferred_element_type=jnp.float32)


def tn_dot(lhs, rhs):
    return lax.dot_general(lhs, rhs, (((0,), (0,)), ((), ())), preferred_element_type=jnp.float32)


def nn_dot(lhs, rhs):
    return lax.dot_general(lhs, rhs, (((1,), (0,)), ((), ())), preferred_element_type=jnp.float32)


def grads_kernel(
    picks, seeds, place, query, out_grad, *rest
):
    pieces = rest[:16]
    query_grad, keep, send_far, send_near = rest[16:20]
    kv, acc, table, signed, kept, dropped_ref, sems = rest[20:]
    item = pl.program_id(0)
    shard = place[0]
    core = place[1]
    head = item // 2
    block = item % 2

    def copies():
        made = []
        for slot in range(SLOTS):
            for half in range(2):
                if slot == 0:
                    kind = half
                else:
                    kind = core if half == 0 else 1 - core
                source = pieces[2 * slot + half]
                if slot == 0:
                    source = source.at[:, pl.ds(pl.multiple_of(place[2], HD), HD)]
                made.append(
                    pltpu.make_async_copy(source, kv.at[slot, kind], sems.at[2 * slot + half])
                )
        return made

    @pl.when(item == 0)
    def _():
        made = copies()
        for copy in made:
            copy.start()
        acc[...] = jnp.zeros_like(acc)
        key_row = lax.broadcasted_iota(jnp.int32, (BLK, BLK), 0)
        query_row = lax.broadcasted_iota(jnp.int32, (BLK, BLK), 1)
        table[...] = (key_row * 9973 + query_row * 40503).astype(jnp.uint32)
        for copy in made:
            copy.wait()

    own = shard * 2 + block
    q = query[...]
    do = out_grad[...]

    def target_of(entry):
        return picks[item, entry]

    dead = [jnp.bool_(False)]
    for entry in range(1, TOPK):
        same = target_of(entry) == target_of(0)
        for other in range(1, entry):
            same = same | (target_of(entry) == target_of(other))
        dead.append(same)

    def kv_rows(entry, kind):
        target = target_of(entry)
        slot = shard - target // 2
        start = pl.multiple_of((target % 2) * BLK, BLK)
        return kv[slot, kind, pl.ds(start, BLK), :]

    def unit_rows(entry, chunk, kind):
        target = target_of(entry)
        slot = shard - target // 2
        start = pl.multiple_of((target % 2) * BLK + chunk * 256, 256)
        return kv[slot, kind, pl.ds(start, 256), :]

    def first_query(entry, chunk):
        return chunk * 256 if entry == 0 else 0

    def fold(value, how):
        return how(value.reshape(256 // 8, 8, value.shape[1]), axis=0)

    units = [(entry, chunk) for entry in range(TOPK) for chunk in range(BLK // 256)]

    def score_dot(entry, chunk):
        lo = first_query(entry, chunk)
        return nt_dot(unit_rows(entry, chunk, 0), q[lo:])

    def widen(value, lo, fill):
        if lo == 0:
            return value
        return jnp.concatenate([jnp.full((8, lo), fill, jnp.float32), value], axis=1)

    def score_rest(entry, chunk, value):
        lo = first_query(entry, chunk)
        if entry == 0:
            key_row = lax.broadcasted_iota(jnp.int32, value.shape, 0)
            query_row = lax.broadcasted_iota(jnp.int32, value.shape, 1)
            value = jnp.where(key_row <= query_row, value, -jnp.inf)
        signed[entry, chunk * 256:(chunk + 1) * 256, lo:] = value
        top = widen(fold(value, jnp.max), lo, -jnp.inf)
        return jnp.where(dead[entry], -jnp.inf, top) if entry else top

    peak = jnp.full((8, BLK), -jnp.inf, jnp.float32)
    ahead = score_dot(*units[0])
    for place_in, unit in enumerate(units):
        value = ahead
        if place_in + 1 < len(units):
            ahead = score_dot(*units[place_in + 1])
        peak = jnp.maximum(peak, score_rest(*unit, value))
    peak = jnp.max(peak, axis=0, keepdims=True)

    def middle_dot(entry, chunk):
        lo = first_query(entry, chunk)
        return nt_dot(unit_rows(entry, chunk, 1), do[lo:])

    def middle_rest(entry, chunk, pgrad):
        lo = first_query(entry, chunk)
        rows = slice(chunk * 256, (chunk + 1) * 256)
        top = peak[:, lo:]
        if entry:
            top = jnp.where(dead[entry], jnp.inf, top)
        e = jnp.exp2((signed[entry, rows, lo:] - top) * (FACTOR * LOG2E))
        base = seeds[head] + own * (BLK * 40503) + target_of(entry) * (BLK * 9973)
        x = table[rows, lo:] + base.astype(jnp.uint32)
        x = x ^ lax.shift_right_logical(x, jnp.uint32(15))
        x = (x * np.uint32((73244475 << 16) % 2**32)) ^ (x * np.uint32((73244475 << 3) % 2**32))
        keeps = x >= np.uint32(DROP_CUT << 16)
        pk = jnp.where(keeps, pgrad, 0.0)
        signed[entry, rows, lo:] = e
        dropped_ref[entry, rows, lo:] = jnp.where(keeps, e, 0.0).astype(jnp.bfloat16)
        kept[entry, rows, lo:] = pk
        return widen(fold(e, jnp.sum), lo, 0.0), widen(fold(e * pk, jnp.sum), lo, 0.0)

    total = delta = jnp.zeros((8, BLK), jnp.float32)
    ahead = middle_dot(*units[0])
    for place_in, unit in enumerate(units):
        value = ahead
        if place_in + 1 < len(units):
            ahead = middle_dot(*units[place_in + 1])
        more_total, more_delta = middle_rest(*unit, value)
        total = total + more_total
        delta = delta + more_delta
    total = jnp.sum(total, axis=0, keepdims=True)
    delta = jnp.sum(delta, axis=0, keepdims=True) / total
    scale = 1.0 / (0.9 * total)
    scale_cols = jnp.transpose(jnp.broadcast_to(scale, (HD, BLK)))
    q_scaled = (q.astype(jnp.float32) * (scale_cols * FACTOR)).astype(jnp.bfloat16)
    do_scaled = (do.astype(jnp.float32) * scale_cols).astype(jnp.bfloat16)

    wide = [(0, 0, 256), (0, 256, 256)] + [(entry, 0, BLK) for entry in range(1, TOPK)]

    def last_rest(entry, start, count):
        lo = start if entry == 0 else 0
        rows = slice(start, start + count)
        weight = signed[entry, rows, lo:]
        sgrad = (weight * (kept[entry, rows, lo:] - delta[:, lo:])).astype(jnp.bfloat16)
        return sgrad, dropped_ref[entry, rows, lo:]

    def last_dots(entry, start, count, sgrad, dropped, qgrad):
        lo = start if entry == 0 else 0
        target = target_of(entry)
        slot = shard - target // 2
        part = (target % 2) * 2 + start // 256
        size = count // 256
        shape = (size, 2, 128, HD)
        acc[slot, 0, pl.ds(part, size)] += nn_dot(sgrad, q_scaled[lo:]).reshape(shape)
        acc[slot, 1, pl.ds(part, size)] += nn_dot(dropped, do_scaled[lo:]).reshape(shape)
        key_start = pl.multiple_of((target % 2) * BLK + start, 256)
        more = tn_dot(kv[slot, 0, pl.ds(key_start, count), :], sgrad)
        if lo:
            return jnp.concatenate([qgrad[:, :lo], qgrad[:, lo:] + more], axis=1)
        return qgrad + more

    qgrad = jnp.zeros((HD, BLK), jnp.float32)
    ahead = last_rest(*wide[0])
    for place_in, unit in enumerate(wide):
        value = ahead
        if place_in + 1 < len(wide):
            ahead = last_rest(*wide[place_in + 1])
        qgrad = last_dots(*unit, *value, qgrad)
    query_grad[...] = jnp.transpose(qgrad * (scale * FACTOR))

    @pl.when(item == ITEMS - 1)
    def _():
        kept_copies = [
            pltpu.make_async_copy(acc.at[slot, :, :, core], keep.at[slot], sems.at[slot])
            for slot in range(SLOTS)
        ]
        for copy in kept_copies:
            copy.start()
        for slot in range(SLOTS):
            group = send_far if slot in FAR else send_near
            index = (FAR if slot in FAR else NEAR).index(slot)
            group[index] = acc[slot, :, :, 1 - core].astype(jnp.bfloat16)
        for copy in kept_copies:
            copy.wait()


def block_grads(query, out_grad, picks, seeds, place, pieces, interpret=False):
    any_spec = pl.BlockSpec(memory_space=pl.ANY)
    item_spec = pl.BlockSpec((BLK, HD), lambda i, *_: (i % 2, i // 2))

    def part(slots, dtype):
        shape = (slots, 2, Y_SIZE, 128, HD)
        return pl.BlockSpec(shape, lambda i, *_: (0, 0, 0, 0, 0)), jax.ShapeDtypeStruct(shape, dtype)

    parts = [
        part(SLOTS, jnp.float32),
        part(len(FAR), jnp.bfloat16),
        part(len(NEAR), jnp.bfloat16),
    ]
    return pl.pallas_call(
        grads_kernel,
        grid_spec=pltpu.PrefetchScalarGridSpec(
            num_scalar_prefetch=3,
            grid=(ITEMS,),
            in_specs=[item_spec, item_spec] + [any_spec] * 16,
            out_specs=[item_spec, any_spec] + [spec for spec, _ in parts[1:]],
            scratch_shapes=[
                pltpu.VMEM((SLOTS, 2, ROWS, HD), jnp.bfloat16),
                pltpu.VMEM((SLOTS, 2, 4, 2, 128, HD), jnp.float32),
                pltpu.VMEM((BLK, BLK), jnp.uint32),
                pltpu.VMEM((TOPK, BLK, BLK), jnp.float32),
                pltpu.VMEM((TOPK, BLK, BLK), jnp.float32),
                pltpu.VMEM((TOPK, BLK, BLK), jnp.bfloat16),
                pltpu.SemaphoreType.DMA((16,)),
            ],
        ),
        out_shape=[jax.ShapeDtypeStruct((ROWS, 4 * HD), jnp.float32)]
        + [shape for _, shape in parts],
        compiler_params=pltpu.CompilerParams(
            vmem_limit_bytes=56 * 1024 * 1024, dimension_semantics=("arbitrary",)
        ),
        name="block_grads",
        interpret=interpret,
    )(picks, seeds, place, query, out_grad, *pieces)


def shifted(array, by):
    pairs = [(i, (i + by) % SEQ_SIZE) for i in range(SEQ_SIZE)]
    return lax.ppermute(array, SEQ_AXES, pairs)


def swapped(array):
    return lax.ppermute(array, "core", [(0, 1), (1, 0)])


def own_kernel(where, keep, other, low, high, *outs):
    for offset in range(Y_SIZE):
        rows = lax.rem(where[0] + offset, Y_SIZE)
        value = keep[0, :, rows] + other[0, :, rows].astype(jnp.float32)
        value = value + low[:, rows].astype(jnp.float32) + high[:, rows].astype(jnp.float32)
        outs[offset][...] = value.astype(outs[offset].dtype)


def own_sums(where, keep, other, low, high):
    def first(count):
        return pl.BlockSpec((count, 2, Y_SIZE, 128, HD), lambda i, *_: (0, 0, 0, 0, 0))

    whole = pl.BlockSpec((2, Y_SIZE, 128, HD), lambda i, *_: (0, 0, 0, 0))
    out = pl.BlockSpec((2, 128, HD), lambda i, *_: (0, 0, 0))
    return pl.pallas_call(
        own_kernel,
        grid_spec=pltpu.PrefetchScalarGridSpec(
            num_scalar_prefetch=1,
            grid=(1,),
            in_specs=[first(1), first(1), whole, whole],
            out_specs=[out] * Y_SIZE,
        ),
        out_shape=[
            jax.ShapeDtypeStruct((2, 128, HD), jnp.bfloat16 if offset else jnp.float32)
            for offset in range(Y_SIZE)
        ],
        name="own_sums",
    )(where, keep, other, low, high)


def spread_kernel(where, *refs):
    key_grad, value_grad = refs[Y_SIZE:]
    for offset in range(Y_SIZE):
        start = pl.multiple_of(lax.rem(where[0] + Y_SIZE - offset, Y_SIZE) * HD, HD)
        key_grad[:, pl.ds(start, HD)] = refs[offset][0].astype(jnp.float32)
        value_grad[:, pl.ds(start, HD)] = refs[offset][1].astype(jnp.float32)


def spread(where, pieces):
    piece = pl.BlockSpec((2, 128, HD), lambda i, *_: (0, 0, 0))
    out = pl.BlockSpec((128, Y_SIZE * HD), lambda i, *_: (0, 0))
    return pl.pallas_call(
        spread_kernel,
        grid_spec=pltpu.PrefetchScalarGridSpec(
            num_scalar_prefetch=1,
            grid=(1,),
            in_specs=[piece] * Y_SIZE,
            out_specs=[out, out],
        ),
        out_shape=[jax.ShapeDtypeStruct((128, Y_SIZE * HD), jnp.float32)] * 2,
        name="spread",
    )(where, *pieces)


def local(query, key, value, out_grad, chosen, drop_seed):
    shard = lax.axis_index(SEQ_AXES)
    core = lax.axis_index("core")
    rank = lax.axis_index("y")
    kv_col = rank * HD
    mine = jnp.where(
        core == 0,
        lax.dynamic_slice_in_dim(key, kv_col, HD, 1),
        lax.dynamic_slice_in_dim(value, kv_col, HD, 1),
    )
    half = ROWS // 2
    got = {}
    got[1] = shifted(mine, 1)
    got[7] = shifted(mine, 7)
    got[2] = shifted(got[1], 1)
    got[6] = shifted(got[7], -1)
    low = shifted(got[2][:half], 2)
    high = shifted(got[6][half:], -2)
    got[3] = shifted(got[2], 1)
    got[5] = shifted(got[6], -1)
    got[4] = jnp.concatenate([low, high])
    pieces = [key, value]
    for slot in range(1, SLOTS):
        pieces += [got[slot], swapped(got[slot])]
    place = jnp.stack([shard, core, kv_col]).astype(jnp.int32)
    query_grad, keep, send_far, send_near = block_grads(
        query, out_grad, chosen.reshape(ITEMS, TOPK), drop_seed, place, pieces
    )
    far = swapped(send_far)
    near = swapped(send_near)

    def total(slot, *more):
        other = far[FAR.index(slot)] if slot in FAR else near[NEAR.index(slot)]
        return sum((p.astype(jnp.float32) for p in more), keep[slot] + other.astype(jnp.float32))

    def rounded(array):
        return array.astype(jnp.bfloat16)

    sent3, sent5, sent4k, sent4v = lax.optimization_barrier(
        (rounded(total(3)), rounded(total(5)), rounded(total(4)[0]), rounded(total(4)[1]))
    )
    from3 = shifted(sent3, -1)
    from5 = shifted(sent5, 1)
    from4k = shifted(sent4k, -2)
    from4v = shifted(sent4v, 2)
    none = jnp.zeros_like(from4k)
    part2 = rounded(total(2, from3, jnp.stack([from4k, none])))
    part6 = rounded(total(6, from5, jnp.stack([none, from4v])))
    part2, part6 = lax.optimization_barrier((part2, part6))
    part1 = rounded(total(1, shifted(part2, -1)))
    part7 = rounded(total(7, shifted(part6, 1)))
    part1, part7 = lax.optimization_barrier((part1, part7))
    from1, from7 = shifted(part1, -1), shifted(part7, -7)
    where = rank.astype(jnp.int32).reshape(1)
    sums = own_sums(where, keep, near, from1, from7)
    pieces = [sums[0]]
    for offset in range(1, Y_SIZE):
        pairs = [(i, (i + offset) % Y_SIZE) for i in range(Y_SIZE)]
        pieces.append(lax.ppermute(sums[offset], "y", pairs))
    key_grad, value_grad = spread(where, pieces)
    return query_grad, key_grad, value_grad


def solution(mesh):
    fine = Mesh(mesh.devices.reshape(4, 8, 4, 2), ("x", "z", "y", "core"))
    seq, head = SEQ_AXES, ("y", "core")
    in_specs = (
        P(seq, head),
        P(seq, None),
        P(seq, None),
        P(seq, head),
        P(head, seq, None),
        P(head),
    )
    out_specs = (P(seq, head), P(seq + head, None), P(seq + head, None))
    return jax.shard_map(local, mesh=fine, in_specs=in_specs, out_specs=out_specs, check_vma=False)
```
